32 devices in a mesh: tm: 4 (over y, x), row: 4 (over z), col: 2 (over core).
Axes of the slice: x: 2, y: 2, z: 4, core: 2. Of those that a mesh axis runs over, the one named last changes fastest.
Arguments:
- blocks: float32 [4, 4096, 4096], P('tm', 'row', 'col'), may hold values from -0.7 to 7.7, as said below
- borders: float32 [4, 640, 4096], P('tm', None, ('row', 'col')), may hold values from -0.3 to 0.3
- arrow_tip: float32 [128, 128], replicated, may hold values from -6 to 6
Outputs:
- schur_blocks: float32 [4, 4096, 4096], P('tm', 'row', 'col')
- factor_panels: float32 [4, 4096, 1024], P('tm', 'row')
- border_out: float32 [4, 640, 4096], P('tm', None, ('row', 'col'))
- tip_out: float32 [128, 128], replicated
The draws below stay inside these ranges and needn't reach their ends.
Inputs may be any that keep to these rules, and one draw needn't show every extreme that they name: `blocks`: each partition's block is symmetric positive definite.
All inputs are finite; a program needn't handle non-finite values.
Results may differ from the reference program's by a relative error of at most 0.0001.
Values sent between devices are 32-bit elements; how exact they have to be, the bound alone decides.
A program may use at most 128 MiB of HBM per device.

```python
import math
import jax
import jax.numpy as jnp
from jax import lax

NODES = 4096
F = 128
P_SIZE = 512
Q = 512
PANELS = 2
PARTITIONS = 4
N_ROW = 4


def draw_blocks(key, part):
    keys = jax.random.split(key, 2)
    noise = jnp.clip(jax.random.normal(keys[0], (PARTITIONS, NODES, NODES), jnp.float32), -5.0, 5.0)
    diag = jax.random.uniform(keys[1], (PARTITIONS, NODES), jnp.float32, 3.0, 6.0)
    noise = (noise + jnp.swapaxes(noise, 1, 2)) * (0.7071068 / math.sqrt(NODES))
    return noise + diag[:, :, None] * jnp.eye(NODES, dtype=jnp.float32)[None]


def shard_levels(own_key, shape, pieces, least, largest):
    factor_of = 1.0
    for position, blocks in pieces:
        heights = jax.random.uniform(jax.random.fold_in(jax.random.fold_in(own_key, 6), position), (blocks,), jnp.float32, least / len(pieces), largest / len(pieces))
        factor_of = factor_of * jnp.repeat(jnp.exp(heights), shape[position] // blocks).reshape((-1,) + (1,) * (len(shape) - 1 - position))
    return factor_of


def gaussian(own_key, dims, scale, most, cuts=(), kind=jnp.bfloat16):
    result = scale * jax.random.normal(own_key, dims, jnp.float32)
    if cuts:
        result = result * shard_levels(own_key, dims, cuts, -0.22, 0.18)
    return jnp.clip(result, -most, most).astype(kind)


def setup_inputs(seed: int = 0) -> dict:
    key_of = jax.random.split(jax.random.key(seed), 4)
    return {
        "blocks": draw_blocks(jax.random.fold_in(key_of[3], 71), 0),
        "borders": gaussian(key_of[1], (PARTITIONS, Q + F, NODES), 0.05, 0.3, ((0, 4), (2, 8)), jnp.float32),
        "arrow_tip": gaussian(key_of[2], (F, F), 1.0, 6.0, (), jnp.float32),
    }


def exact_dot(left, right):
    return jnp.dot(left.astype(jnp.float32), right.astype(jnp.float32), precision=lax.Precision.HIGHEST, preferred_element_type=jnp.float32)

def right_solve(chol, values):
    return lax.linalg.triangular_solve(chol, values, left_side=False, lower=True, transpose_a=True)

def panel_nodes(k):
    slice_width = P_SIZE // N_ROW
    starts = jnp.arange(N_ROW, dtype=jnp.int32)[:, None] * (NODES // N_ROW) + k * slice_width
    return (starts + jnp.arange(slice_width, dtype=jnp.int32)[None, :]).reshape(-1)

def one_partition(inputs):
    block, border = inputs
    offsets = jnp.arange(NODES, dtype=jnp.int32) % (NODES // N_ROW)
    handoff = jnp.zeros((Q + F, Q), jnp.float32)
    tip_term = jnp.zeros((F, F), jnp.float32)
    factors = []
    for k in range(PANELS):
        nodes = panel_nodes(k)
        panel = jnp.take(block, nodes, axis=1)
        corner = jnp.take(panel, nodes, axis=0)
        chol = jnp.linalg.cholesky(corner)
        rows = right_solve(chol, panel)
        rows = jnp.where((offsets < k * (P_SIZE // N_ROW))[:, None], jnp.float32(0.0), rows)
        arrow = right_solve(chol, jnp.take(border, nodes, axis=1))
        block = block - exact_dot(rows, rows.T)
        border = border - exact_dot(arrow, rows.T)
        handoff = handoff + exact_dot(arrow, arrow[:Q].T)
        tip_term = tip_term + exact_dot(arrow[Q:], arrow[Q:].T)
        factors.append(rows)
    return (block, jnp.concatenate(factors, axis=1), border, handoff, tip_term)

def reference(blocks, borders, arrow_tip):
    new_blocks, factors, new_borders, handoffs, tip_terms = lax.map(one_partition, (blocks, borders))
    received = jnp.concatenate([jnp.zeros((1, Q + F, Q), jnp.float32), handoffs[:-1]], axis=0)
    new_blocks = new_blocks.at[:, NODES - Q:, NODES - Q:].add(-received[:, :Q])
    new_borders = new_borders.at[:, Q:, NODES - Q:].add(-received[:, Q:])
    tip_out = arrow_tip - jnp.sum(tip_terms, axis=0)
    return (new_blocks, factors, new_borders, tip_out)
```

```python
import jax
import jax.numpy as jnp
from jax import lax
from jax.experimental import pallas as pl
from jax.experimental.pallas import tpu as pltpu
from jax.sharding import PartitionSpec as P

F = 128
P_SIZE = 512
Q = 512
PANELS = 2
BLOCK = 128
TILE = 16


def mm(left, right, precision=lax.Precision.HIGH):
    return jnp.dot(left, right, precision=precision, preferred_element_type=jnp.float32)


def dot_full(left, right):
    return lax.dot_general(
        left, right, (((1,), (0,)), ((), ())),
        precision=lax.Precision.HIGHEST, preferred_element_type=jnp.float32,
    )


def dot_first(left, right):
    return lax.dot_general(
        left, right, (((0,), (0,)), ((), ())),
        precision=lax.Precision.HIGHEST, preferred_element_type=jnp.float32,
    )


def inverse_factor_kernel(corner_ref, out_ref, work, pair):
    size = corner_ref.shape[0]
    work[...] = corner_ref[...]
    out_ref[...] = jnp.zeros_like(out_ref)
    row_of = lax.broadcasted_iota(jnp.int32, (BLOCK, BLOCK), 0)
    col_of = lax.broadcasted_iota(jnp.int32, (BLOCK, BLOCK), 1)
    eye = (row_of == col_of).astype(jnp.float32)
    sub = lax.broadcasted_iota(jnp.int32, (TILE, BLOCK), 0)
    deep = lax.broadcasted_iota(jnp.int32, (BLOCK, 2 * BLOCK), 0)

    def tile_step(t, carry):
        start = pl.multiple_of(t * TILE, TILE)
        left = pair[pl.ds(start, TILE), :BLOCK]
        right = pair[pl.ds(start, TILE), BLOCK:]
        turned = pltpu.roll(left, BLOCK - start, axis=1)
        lanes = [jnp.broadcast_to(turned[:, s : s + 1], (TILE, BLOCK)) for s in range(TILE)]
        for s in range(TILE):
            scale = lax.rsqrt(lanes[s][s : s + 1, :])
            coef = jnp.where(sub > s, lanes[s] * scale, 0.0)
            row_l = left[s : s + 1, :] * scale
            row_r = right[s : s + 1, :] * scale
            for u in range(s + 1, TILE):
                lanes[u] = lanes[u] - coef * (lanes[u][s : s + 1, :] * scale)
            left = jnp.where(sub == s, row_l, left - coef * row_l)
            right = jnp.where(sub == s, row_r, right - coef * row_r)
        pair[pl.ds(start, TILE), :BLOCK] = left
        pair[pl.ds(start, TILE), BLOCK:] = right
        both = jnp.concatenate([left, right], axis=1)
        change = dot_first(left, both)
        pair[...] = pair[...] - jnp.where(deep >= start + TILE, change, 0.0)
        return carry

    for b in range(size // BLOCK):
        lo, hi = b * BLOCK, (b + 1) * BLOCK
        pair[:, :BLOCK] = work[lo:hi, lo:hi]
        pair[:, BLOCK:] = eye
        lax.fori_loop(0, BLOCK // TILE, tile_step, 0)
        inv = pair[:, BLOCK:]
        if lo:
            done = dot_full(inv, out_ref[lo:hi, :lo])
            out_ref[lo:hi, :lo] = done
        out_ref[lo:hi, lo:hi] = inv
        if hi < size:
            across = dot_full(inv, work[lo:hi, hi:])
            work[hi:, hi:] = work[hi:, hi:] - dot_first(across, across)
            out_ref[hi:, :hi] = out_ref[hi:, :hi] - dot_first(across, out_ref[lo:hi, :hi])


def inverse_factor(corner):
    size = corner.shape[0]
    return pl.pallas_call(
        inverse_factor_kernel,
        out_shape=jax.ShapeDtypeStruct(corner.shape, jnp.float32),
        in_specs=[pl.BlockSpec(memory_space=pltpu.VMEM)],
        out_specs=pl.BlockSpec(memory_space=pltpu.VMEM),
        scratch_shapes=[
            pltpu.VMEM((size, size), jnp.float32),
            pltpu.VMEM((BLOCK, 2 * BLOCK), jnp.float32),
        ],
        cost_estimate=pl.CostEstimate(
            flops=60000 * size * size // 8, bytes_accessed=8 * size * size, transcendentals=size
        ),
        compiler_params=pltpu.CompilerParams(vmem_limit_bytes=24 * 1024 * 1024),
    )(corner)


def shards(blocks, borders, arrow_tip):
    block = blocks[0]
    border = borders[0]
    n_tm = lax.axis_size("tm")
    n_row = lax.axis_size("row")
    n_col = lax.axis_size("col")
    row_id = lax.axis_index("row")
    col_id = lax.axis_index("col")
    rows_dev, cols_dev = block.shape
    border_rows, width = border.shape
    piece = P_SIZE // n_row
    per_col = n_row // n_col
    target = jnp.logical_and(row_id == n_row - 1, col_id == n_col - 1)

    def panel_columns(rows, k):
        return jnp.concatenate(
            [
                rows[:, j * rows_dev + k * piece : j * rows_dev + (k + 1) * piece]
                for j in range(per_col)
            ],
            axis=1,
        )

    corners = []
    for k in range(PANELS):
        mine = block[k * piece : (k + 1) * piece]
        mine = jnp.concatenate([panel_columns(mine, i) for i in range(k + 1)], axis=1)
        every = lax.all_gather(mine, ("row", "col"), axis=0, tiled=False)
        every = every.reshape(n_row, n_col, piece, k + 1, per_col * piece)
        every = jnp.transpose(every, (3, 0, 2, 1, 4)).reshape(k + 1, P_SIZE, P_SIZE)
        corners.append(every)

    sides = [
        lax.all_gather(panel_columns(block, k), "col", axis=1, tiled=True) for k in range(PANELS)
    ]
    tops = [
        lax.all_gather(block[k * piece : (k + 1) * piece], "row", axis=0, tiled=True)
        for k in range(PANELS)
    ]
    share = border_rows // n_col
    held = border[:, : PANELS * piece]
    part = held[:share]
    for c in range(1, n_col):
        sent = lax.ppermute(held[c * share : (c + 1) * share], "col", [(0, c)])
        part = jnp.where(col_id == c, sent, part)
    edges = lax.all_gather(part, ("row", "col"), axis=0, tiled=False)
    edges = edges.reshape(n_row, n_col, share, PANELS, piece)
    edges = jnp.transpose(edges, (3, 1, 2, 0, 4)).reshape(PANELS, border_rows, P_SIZE)

    inverses = []
    below = [[None] * PANELS for _ in range(PANELS)]
    for k in range(PANELS):
        corner = corners[k][k]
        for i in range(k):
            left = corners[k][i]
            for j in range(i):
                left = left - mm(below[k][j], below[i][j].T, lax.Precision.HIGHEST)
            below[k][i] = mm(left, inverses[i].T, lax.Precision.HIGHEST)
            corner = corner - mm(below[k][i], below[k][i].T, lax.Precision.HIGHEST)
        inverses.append(inverse_factor(corner))

    arrows, rows, columns = [], [], []
    for k in range(PANELS):
        edge = edges[k]
        for i in range(k):
            edge = edge - mm(arrows[i], below[k][i].T)
        arrows.append(mm(edge, inverses[k].T))
    arrow = jnp.concatenate(arrows, axis=1)
    handoff = mm(arrow, arrow[:Q].T)
    tip = mm(arrow[Q:], arrow[Q:].T)
    incoming = lax.ppermute(handoff, "tm", [(t, t + 1) for t in range(n_tm - 1)])
    tip_out = arrow_tip - lax.psum(tip, "tm")

    node = jnp.arange(rows_dev, dtype=jnp.int32)
    node_col = jnp.arange(cols_dev, dtype=jnp.int32) % rows_dev
    for k in range(PANELS):
        side, top = sides[k], tops[k]
        for i in range(k):
            side = side - mm(rows[i], below[k][i].T)
            top = top - mm(below[k][i], columns[i])
        side = mm(side, inverses[k].T)
        top = mm(inverses[k], top)
        if k:
            side = jnp.where((node < k * piece)[:, None], jnp.float32(0.0), side)
            top = jnp.where((node_col < k * piece)[None, :], jnp.float32(0.0), top)
        rows.append(side)
        columns.append(top)
    factor = jnp.concatenate(rows, axis=1)
    own = lax.dynamic_slice_in_dim(factor, col_id * width, width, 0)
    block = block - mm(factor, jnp.concatenate(columns, axis=0))
    border = border - mm(arrow, own.T)
    taken = jnp.where(target, incoming, jnp.float32(0.0))
    block = block.at[rows_dev - Q :, cols_dev - Q :].add(-taken[:Q])
    border = border.at[Q:, width - Q :].add(-taken[Q:])
    return (block[None], factor[None], border[None], tip_out)


def solution(mesh):
    placed = (P("tm", "row", "col"), P("tm", None, ("row", "col")), P())
    return jax.shard_map(
        shards,
        mesh=mesh,
        in_specs=placed,
        out_specs=(P("tm", "row", "col"), P("tm", "row", None), P("tm", None, ("row", "col")), P()),
        check_vma=False,
    )
```

```python
import jax
import jax.numpy as jnp
from jax import lax
from jax.experimental import pallas as pl
from jax.experimental.pallas import tpu as pltpu
from jax.sharding import PartitionSpec as P

F = 128
P_SIZE = 512
Q = 512
PANELS = 2
BLOCK = 128
TILE = 16


def mm(left, right, precision=lax.Precision.HIGH):
    return jnp.dot(left, right, precision=precision, preferred_element_type=jnp.float32)


def dot_full(left, right):
    return lax.dot_general(
        left, right, (((1,), (0,)), ((), ())),
        precision=lax.Precision.HIGHEST, preferred_element_type=jnp.float32,
    )


def dot_first(left, right):
    return lax.dot_general(
        left, right, (((0,), (0,)), ((), ())),
        precision=lax.Precision.HIGHEST, preferred_element_type=jnp.float32,
    )


def inverse_factor_kernel(corner_ref, out_ref, work, pair):
    size = corner_ref.shape[0]
    work[...] = corner_ref[...]
    out_ref[...] = jnp.zeros_like(out_ref)
    row_of = lax.broadcasted_iota(jnp.int32, (BLOCK, BLOCK), 0)
    col_of = lax.broadcasted_iota(jnp.int32, (BLOCK, BLOCK), 1)
    eye = (row_of == col_of).astype(jnp.float32)
    sub = lax.broadcasted_iota(jnp.int32, (TILE, BLOCK), 0)
    deep = lax.broadcasted_iota(jnp.int32, (BLOCK, 2 * BLOCK), 0)

    def tile_step(t, carry):
        start = pl.multiple_of(t * TILE, TILE)
        left = pair[pl.ds(start, TILE), :BLOCK]
        right = pair[pl.ds(start, TILE), BLOCK:]
        turned = pltpu.roll(left, BLOCK - start, axis=1)
        lanes = [jnp.broadcast_to(turned[:, s : s + 1], (TILE, BLOCK)) for s in range(TILE)]
        for s in range(TILE):
            scale = lax.rsqrt(lanes[s][s : s + 1, :])
            coef = jnp.where(sub > s, lanes[s] * scale, 0.0)
            row_l = left[s : s + 1, :] * scale
            row_r = right[s : s + 1, :] * scale
            for u in range(s + 1, TILE):
                lanes[u] = lanes[u] - coef * (lanes[u][s : s + 1, :] * scale)
            left = jnp.where(sub == s, row_l, left - coef * row_l)
            right = jnp.where(sub == s, row_r, right - coef * row_r)
        pair[pl.ds(start, TILE), :BLOCK] = left
        pair[pl.ds(start, TILE), BLOCK:] = right
        both = jnp.concatenate([left, right], axis=1)
        change = dot_first(left, both)
        pair[...] = pair[...] - jnp.where(deep >= start + TILE, change, 0.0)
        return carry

    for b in range(size // BLOCK):
        lo, hi = b * BLOCK, (b + 1) * BLOCK
        pair[:, :BLOCK] = work[lo:hi, lo:hi]
        pair[:, BLOCK:] = eye
        lax.fori_loop(0, BLOCK // TILE, tile_step, 0)
        inv = pair[:, BLOCK:]
        if lo:
            done = dot_full(inv, out_ref[lo:hi, :lo])
            out_ref[lo:hi, :lo] = done
        out_ref[lo:hi, lo:hi] = inv
        if hi < size:
            across = dot_full(inv, work[lo:hi, hi:])
            work[hi:, hi:] = work[hi:, hi:] - dot_first(across, across)
            out_ref[hi:, :hi] = out_ref[hi:, :hi] - dot_first(across, out_ref[lo:hi, :hi])


def inverse_factor(corner):
    size = corner.shape[0]
    return pl.pallas_call(
        inverse_factor_kernel,
        out_shape=jax.ShapeDtypeStruct(corner.shape, jnp.float32),
        in_specs=[pl.BlockSpec(memory_space=pltpu.VMEM)],
        out_specs=pl.BlockSpec(memory_space=pltpu.VMEM),
        scratch_shapes=[
            pltpu.VMEM((size, size), jnp.float32),
            pltpu.VMEM((BLOCK, 2 * BLOCK), jnp.float32),
        ],
        cost_estimate=pl.CostEstimate(
            flops=90000 * size * size, bytes_accessed=8 * size * size, transcendentals=size
        ),
        compiler_params=pltpu.CompilerParams(vmem_limit_bytes=24 * 1024 * 1024),
    )(corner)


def shards(blocks, borders, arrow_tip):
    block = blocks[0]
    border = borders[0]
    n_tm = lax.axis_size("tm")
    n_row = lax.axis_size("row")
    n_col = lax.axis_size("col")
    row_id = lax.axis_index("row")
    col_id = lax.axis_index("col")
    rows_dev, cols_dev = block.shape
    border_rows, width = border.shape
    piece = P_SIZE // n_row
    per_col = n_row // n_col
    target = jnp.logical_and(row_id == n_row - 1, col_id == n_col - 1)

    def panel_columns(rows, k):
        return jnp.concatenate(
            [
                rows[:, j * rows_dev + k * piece : j * rows_dev + (k + 1) * piece]
                for j in range(per_col)
            ],
            axis=1,
        )

    def over_col(value):
        parts = [value]
        for step in range(1, n_col):
            turn = [(c, (c + step) % n_col) for c in range(n_col)]
            parts.append(lax.ppermute(value, "col", turn))
        ordered = []
        for c in range(n_col):
            away = lax.rem(col_id - c + n_col, n_col)
            chosen = parts[0]
            for step in range(1, n_col):
                chosen = jnp.where(away == step, parts[step], chosen)
            ordered.append(chosen)
        return jnp.concatenate(ordered, axis=1)

    first = lax.all_gather(panel_columns(block[:piece], 0), ("row", "col"), axis=0, tiled=False)
    first = first.reshape(n_row, n_col, piece, per_col * piece)
    first = jnp.transpose(first, (0, 2, 1, 3)).reshape(P_SIZE, P_SIZE)
    sides = [over_col(panel_columns(block, k)) for k in range(PANELS)]
    tops = [
        lax.all_gather(block[k * piece : (k + 1) * piece], "row", axis=0, tiled=True)
        for k in range(PANELS)
    ]
    corners = [[first]]
    for k in range(1, PANELS):
        corners.append([over_col(panel_columns(tops[k], i)) for i in range(k + 1)])
    share = border_rows // n_col
    held = border[:, : PANELS * piece]
    part = held[:share]
    for c in range(1, n_col):
        sent = lax.ppermute(held[c * share : (c + 1) * share], "col", [(0, c)])
        part = jnp.where(col_id == c, sent, part)
    edges = lax.all_gather(part, ("row", "col"), axis=0, tiled=False)
    edges = edges.reshape(n_row, n_col, share, PANELS, piece)
    edges = jnp.transpose(edges, (3, 1, 2, 0, 4)).reshape(PANELS, border_rows, P_SIZE)

    inverses = []
    below = [[None] * PANELS for _ in range(PANELS)]
    for k in range(PANELS):
        corner = corners[k][k]
        for i in range(k):
            left = corners[k][i]
            for j in range(i):
                left = left - mm(below[k][j], below[i][j].T, lax.Precision.HIGHEST)
            below[k][i] = mm(left, inverses[i].T, lax.Precision.HIGHEST)
            corner = corner - mm(below[k][i], below[k][i].T, lax.Precision.HIGHEST)
        inverses.append(inverse_factor(corner))

    arrows, rows, columns = [], [], []
    for k in range(PANELS):
        edge = edges[k]
        for i in range(k):
            edge = edge - mm(arrows[i], below[k][i].T)
        arrows.append(mm(edge, inverses[k].T))
    arrow = jnp.concatenate(arrows, axis=1)
    handoff = mm(arrow, arrow[:Q].T)
    tip = mm(arrow[Q:], arrow[Q:].T)
    incoming = lax.ppermute(handoff, "tm", [(t, t + 1) for t in range(n_tm - 1)])
    tip, tops[0] = lax.optimization_barrier((tip, tops[0]))
    tip_out = arrow_tip - lax.psum(tip, "tm")

    node = jnp.arange(rows_dev, dtype=jnp.int32)
    node_col = jnp.arange(cols_dev, dtype=jnp.int32) % rows_dev
    for k in range(PANELS):
        side, top = sides[k], tops[k]
        for i in range(k):
            side = side - mm(rows[i], below[k][i].T)
            top = top - mm(below[k][i], columns[i])
        side = mm(side, inverses[k].T)
        top = mm(inverses[k], top)
        if k:
            side = jnp.where((node < k * piece)[:, None], jnp.float32(0.0), side)
            top = jnp.where((node_col < k * piece)[None, :], jnp.float32(0.0), top)
        rows.append(side)
        columns.append(top)
    factor = jnp.concatenate(rows, axis=1)
    own = lax.dynamic_slice_in_dim(factor, col_id * width, width, 0)
    block = block - mm(factor, jnp.concatenate(columns, axis=0))
    border = border - mm(arrow, own.T)
    taken = jnp.where(target, incoming, jnp.float32(0.0))
    block = block.at[rows_dev - Q :, cols_dev - Q :].add(-taken[:Q])
    border = border.at[Q:, width - Q :].add(-taken[Q:])
    return (block[None], factor[None], border[None], tip_out)


def solution(mesh):
    placed = (P("tm", "row", "col"), P("tm", None, ("row", "col")), P())
    return jax.shard_map(
        shards,
        mesh=mesh,
        in_specs=placed,
        out_specs=(P("tm", "row", "col"), P("tm", "row", None), P("tm", None, ("row", "col")), P()),
        check_vma=False,
    )
```

```python
import jax
import jax.numpy as jnp
from jax import lax
from jax.experimental import pallas as pl
from jax.experimental.pallas import tpu as pltpu
from jax.sharding import PartitionSpec as P

F = 128
P_SIZE = 512
Q = 512
PANELS = 2
BLOCK = 128
TILE = 16


def mm(left, right, precision=lax.Precision.HIGH):
    return jnp.dot(left, right, precision=precision, preferred_element_type=jnp.float32)


def dot_full(left, right):
    return lax.dot_general(
        left, right, (((1,), (0,)), ((), ())),
        precision=lax.Precision.HIGHEST, preferred_element_type=jnp.float32,
    )


def dot_first(left, right):
    return lax.dot_general(
        left, right, (((0,), (0,)), ((), ())),
        precision=lax.Precision.HIGHEST, preferred_element_type=jnp.float32,
    )


def inverse_factor_kernel(corner_ref, out_ref, work, pair):
    size = corner_ref.shape[0]
    work[...] = corner_ref[...]
    out_ref[...] = jnp.zeros_like(out_ref)
    row_of = lax.broadcasted_iota(jnp.int32, (BLOCK, BLOCK), 0)
    col_of = lax.broadcasted_iota(jnp.int32, (BLOCK, BLOCK), 1)
    eye = (row_of == col_of).astype(jnp.float32)
    sub = lax.broadcasted_iota(jnp.int32, (TILE, BLOCK), 0)
    deep = lax.broadcasted_iota(jnp.int32, (BLOCK, 2 * BLOCK), 0)

    def tile_step(t, carry):
        start = pl.multiple_of(t * TILE, TILE)
        left = pair[pl.ds(start, TILE), :BLOCK]
        right = pair[pl.ds(start, TILE), BLOCK:]
        turned = pltpu.roll(left, BLOCK - start, axis=1)
        lanes = [jnp.broadcast_to(turned[:, s : s + 1], (TILE, BLOCK)) for s in range(TILE)]
        for s in range(TILE):
            scale = lax.rsqrt(lanes[s][s : s + 1, :])
            coef = jnp.where(sub > s, lanes[s] * scale, 0.0)
            row_l = left[s : s + 1, :] * scale
            row_r = right[s : s + 1, :] * scale
            for u in range(s + 1, TILE):
                lanes[u] = lanes[u] - coef * (lanes[u][s : s + 1, :] * scale)
            left = jnp.where(sub == s, row_l, left - coef * row_l)
            right = jnp.where(sub == s, row_r, right - coef * row_r)
        pair[pl.ds(start, TILE), :BLOCK] = left
        pair[pl.ds(start, TILE), BLOCK:] = right
        both = jnp.concatenate([left, right], axis=1)
        change = dot_first(left, both)
        pair[...] = pair[...] - jnp.where(deep >= start + TILE, change, 0.0)
        return carry

    for b in range(size // BLOCK):
        lo, hi = b * BLOCK, (b + 1) * BLOCK
        pair[:, :BLOCK] = work[lo:hi, lo:hi]
        pair[:, BLOCK:] = eye
        lax.fori_loop(0, BLOCK // TILE, tile_step, 0)
        inv = pair[:, BLOCK:]
        if lo:
            done = dot_full(inv, out_ref[lo:hi, :lo])
            out_ref[lo:hi, :lo] = done
        out_ref[lo:hi, lo:hi] = inv
        if hi < size:
            across = dot_full(inv, work[lo:hi, hi:])
            work[hi:, hi:] = work[hi:, hi:] - dot_first(across, across)
            out_ref[hi:, :hi] = out_ref[hi:, :hi] - dot_first(across, out_ref[lo:hi, :hi])


def inverse_factor(corner):
    size = corner.shape[0]
    return pl.pallas_call(
        inverse_factor_kernel,
        out_shape=jax.ShapeDtypeStruct(corner.shape, jnp.float32),
        in_specs=[pl.BlockSpec(memory_space=pltpu.VMEM)],
        out_specs=pl.BlockSpec(memory_space=pltpu.VMEM),
        scratch_shapes=[
            pltpu.VMEM((size, size), jnp.float32),
            pltpu.VMEM((BLOCK, 2 * BLOCK), jnp.float32),
        ],
        cost_estimate=pl.CostEstimate(
            flops=90000 * size * size, bytes_accessed=8 * size * size, transcendentals=size
        ),
        compiler_params=pltpu.CompilerParams(vmem_limit_bytes=24 * 1024 * 1024),
    )(corner)


def shards(blocks, borders, arrow_tip):
    block = blocks[0]
    border = borders[0]
    n_tm = lax.axis_size("tm")
    n_row = lax.axis_size("row")
    n_col = lax.axis_size("col")
    row_id = lax.axis_index("row")
    col_id = lax.axis_index("col")
    rows_dev, cols_dev = block.shape
    border_rows, width = border.shape
    piece = P_SIZE // n_row
    per_col = n_row // n_col
    target = jnp.logical_and(row_id == n_row - 1, col_id == n_col - 1)

    def panel_columns(rows, k):
        return jnp.concatenate(
            [
                rows[:, j * rows_dev + k * piece : j * rows_dev + (k + 1) * piece]
                for j in range(per_col)
            ],
            axis=1,
        )

    def over_col(value):
        parts = [value]
        for step in range(1, n_col):
            turn = [(c, (c + step) % n_col) for c in range(n_col)]
            parts.append(lax.ppermute(value, "col", turn))
        ordered = []
        for c in range(n_col):
            away = lax.rem(col_id - c + n_col, n_col)
            chosen = parts[0]
            for step in range(1, n_col):
                chosen = jnp.where(away == step, parts[step], chosen)
            ordered.append(chosen)
        return jnp.concatenate(ordered, axis=1)

    first = lax.all_gather(panel_columns(block[:piece], 0), ("row", "col"), axis=0, tiled=False)
    first = first.reshape(n_row, n_col, piece, per_col * piece)
    first = jnp.transpose(first, (0, 2, 1, 3)).reshape(P_SIZE, P_SIZE)
    sides = [over_col(panel_columns(block, k)) for k in range(PANELS)]
    turned = [block[:piece]]
    sources = [row_id]
    for step in range(1, n_row):
        turn = [(r, (r + step) % n_row) for r in range(n_row)]
        turned.append(lax.ppermute(block[:piece], "row", turn))
        sources.append(lax.rem(row_id - step + n_row, n_row))
    tops = [jnp.concatenate(turned, axis=0)] + [
        lax.all_gather(block[k * piece : (k + 1) * piece], "row", axis=0, tiled=True)
        for k in range(1, PANELS)
    ]
    share = border_rows // n_col
    held = border[:, : PANELS * piece]
    part = held[:share]
    for c in range(1, n_col):
        sent = lax.ppermute(held[c * share : (c + 1) * share], "col", [(0, c)])
        part = jnp.where(col_id == c, sent, part)
    part, tops[-1] = lax.optimization_barrier((part, tops[-1]))
    edges = lax.all_gather(part, ("row", "col"), axis=0, tiled=False)
    edges = edges.reshape(n_row, n_col, share, PANELS, piece)
    edges = jnp.transpose(edges, (3, 1, 2, 0, 4)).reshape(PANELS, border_rows, P_SIZE)

    corners = [[first]]
    for k in range(1, PANELS):
        corners.append([over_col(panel_columns(tops[k], i)) for i in range(k + 1)])

    inverses = []
    below = [[None] * PANELS for _ in range(PANELS)]
    for k in range(PANELS):
        corner = corners[k][k]
        for i in range(k):
            left = corners[k][i]
            for j in range(i):
                left = left - mm(below[k][j], below[i][j].T, lax.Precision.HIGHEST)
            below[k][i] = mm(left, inverses[i].T, lax.Precision.HIGHEST)
            corner = corner - mm(below[k][i], below[k][i].T, lax.Precision.HIGHEST)
        inverses.append(inverse_factor(corner))

    arrows, rows, columns = [], [], []
    for k in range(PANELS):
        edge = edges[k]
        for i in range(k):
            edge = edge - mm(arrows[i], below[k][i].T)
        arrows.append(mm(edge, inverses[k].T))
    arrow = jnp.concatenate(arrows, axis=1)
    handoff = mm(arrow, arrow[:Q].T)
    tip = mm(arrow[Q:], arrow[Q:].T)
    incoming = lax.ppermute(handoff, "tm", [(t, t + 1) for t in range(n_tm - 1)])
    tip_out = arrow_tip - lax.psum(tip, "tm")

    node = jnp.arange(rows_dev, dtype=jnp.int32)
    node_col = jnp.arange(cols_dev, dtype=jnp.int32) % rows_dev
    for k in range(PANELS):
        side, top = sides[k], tops[k]
        for i in range(k):
            side = side - mm(rows[i], below[k][i].T)
            top = top - mm(below[k][i], columns[i])
        side = mm(side, inverses[k].T)
        inverse = inverses[k]
        if k == 0:
            inverse = jnp.concatenate(
                [lax.dynamic_slice_in_dim(inverse, r * piece, piece, 1) for r in sources], axis=1
            )
        top = mm(inverse, top)
        if k:
            side = jnp.where((node < k * piece)[:, None], jnp.float32(0.0), side)
            top = jnp.where((node_col < k * piece)[None, :], jnp.float32(0.0), top)
        rows.append(side)
        columns.append(top)
    factor = jnp.concatenate(rows, axis=1)
    own = lax.dynamic_slice_in_dim(factor, col_id * width, width, 0)
    block = block - mm(factor, jnp.concatenate(columns, axis=0))
    border = border - mm(arrow, own.T)
    taken = jnp.where(target, incoming, jnp.float32(0.0))
    block = block.at[rows_dev - Q :, cols_dev - Q :].add(-taken[:Q])
    border = border.at[Q:, width - Q :].add(-taken[Q:])
    return (block[None], factor[None], border[None], tip_out)


def solution(mesh):
    placed = (P("tm", "row", "col"), P("tm", None, ("row", "col")), P())
    return jax.shard_map(
        shards,
        mesh=mesh,
        in_specs=placed,
        out_specs=(P("tm", "row", "col"), P("tm", "row", None), P("tm", None, ("row", "col")), P()),
        check_vma=False,
    )
```
